32 devices in a mesh: dp: 16 (over z, y, x), tensor: 2 (over core).
Axes of the slice: x: 2, y: 2, z: 4, core: 2. Of those that a mesh axis runs over, the one named last changes fastest.
Arguments:
- tokens: bfloat16 [16, 1024, 768], P('dp'), may hold values from -6 to 6
- gain_attn: float32 [768], replicated, may hold values from 0.5 to 1.5
- query_key_value_weight: bfloat16 [3, 768, 768], P(None, None, 'tensor'), may hold values from -0.21875 to 0.21875
- attn_out_weight: bfloat16 [768, 768], P('tensor'), may hold values from -0.875 to 0.875
- position_bias_matrix: float32 [32, 12], P(None, 'tensor'), may hold values from -4 to 4
- gain_expert: float32 [768], replicated, may hold values from 0.5 to 1.5
- router: float32 [768, 4], replicated, may hold values from -0.21875 to 0.21875
- expert_in: bfloat16 [4, 768, 3072], P(None, None, 'tensor'), may hold values from -0.21875 to 0.21875
- expert_out: bfloat16 [4, 3072, 768], P(None, 'tensor'), may hold values from -0.4375 to 0.4375
- segments: int32 [16, 1024], P('dp'), may hold values from 0 to 3, never falling along the last dimension, each value on 1 to 512 neighbouring positions
- routes: int32 [16, 1024], P('dp'), may hold values from 0 to 3, as said below
- slots: int32 [16, 1024], P('dp'), may hold values from 0 to 319, as said below
- cotangent: bfloat16 [16, 1024, 768], P('dp'), may hold values from -6 to 6
Outputs:
- output: bfloat16 [16, 1024, 768], P('dp')
- grad_tokens: float32 [16, 1024, 768], P('dp')
- grad_gain_attn: float32 [768], P('dp')
- projection_weight_gradient: float32 [3, 768, 768], P(None, 'dp', 'tensor')
- grad_attn_out: float32 [768, 768], P('tensor', 'dp')
- grad_bias_table: float32 [32, 12], P(None, 'tensor')
- grad_gain_expert: float32 [768], P('dp')
- grad_router: float32 [768, 4], P('dp')
- grad_expert_in: float32 [4, 768, 3072], P(None, 'dp', 'tensor')
- grad_expert_out: float32 [4, 3072, 768], P(None, 'tensor', 'dp')
The draws below stay inside these ranges and needn't reach their ends.
Inputs may be any that keep to these rules, and one draw needn't show every extreme that they name: `routes`: within each aligned block of 1 sequence no two tokens have both the same route and the same slot, so an expert holds at most 320 tokens of a block; in every block some expert holds exactly 320. `slots`: paired with routes as stated there.
All inputs are finite; a program needn't handle non-finite values.
Results may differ from the reference program's by a relative error of at most 0.02.
Values may be sent and summed in bfloat16 or wider, within the bound.
A program may use at most 320 MiB of HBM per device.

```python
import math
from functools import partial
import jax
import jax.numpy as jnp
import numpy as np
from jax import lax

D = 768
HEADS = 12
HEAD_DIM = 64
FF = 3072
BUCKETS = 32
EXPERTS = 4
SEQ = 1024
SEQS_DEV = 1
CAP = 320
BATCH = 16
N_TENSOR = 2


def slot_places(key):
    blocks = BATCH // SEQS_DEV
    rows = SEQS_DEV * SEQ

    def one_block(index):
        sub = jax.random.fold_in(key, index)
        first_key, second_key, third_key = jax.random.split(sub, 3)
        filled = jax.random.randint(first_key, (), 0, EXPERTS).astype(jnp.int32)
        others = jax.random.permutation(second_key, (EXPERTS - 1) * CAP).astype(jnp.int32)
        owner = others // CAP
        owner = owner + (owner >= filled).astype(jnp.int32)
        places = owner * CAP + others % CAP
        full_row = filled * CAP + jnp.arange(CAP, dtype=jnp.int32)
        chosen = jnp.concatenate([full_row, places[:rows - CAP]])
        return jax.random.permutation(third_key, chosen)
    return jax.vmap(one_block)(jnp.arange(blocks, dtype=jnp.int32)).reshape(BATCH, SEQ)


def draw_routes(key, part):
    return (slot_places(key) // CAP).astype(jnp.int32)


def draw_slots(key, part):
    return (slot_places(key) % CAP).astype(jnp.int32)


def level_of(own_key, extent, cuts, least, largest):
    def one(position, shards_of):
        heights = jax.random.uniform(jax.random.fold_in(jax.random.fold_in(own_key, 6), position), (shards_of,), jnp.float32, least / len(cuts), largest / len(cuts))
        return jnp.repeat(jnp.exp(heights), extent[position] // shards_of).reshape((-1,) + (1,) * (len(extent) - position - 1))

    level = one(*cuts[0])
    for cut in cuts[1:]:
        level = level * one(*cut)
    return level


def profile(number_of, total, most, skew):
    weights = [(1 << 20) // math.isqrt(grade ** skew) + 1 for grade in range(2, number_of + 1)]
    spare, holding = total - most - (number_of - 1), [1] * (number_of - 1)
    while spare > 0:
        movable = [i for i in range(number_of - 1) if holding[i] < most]
        pool, remaining = sum([weights[i] for i in movable]), spare
        for i in movable:
            addition = min(most - holding[i], max(1, remaining * weights[i] // pool), spare)
            holding[i] = holding[i] + addition
            spare = spare - addition
    return np.array([most] + holding)


def ragged(own_key, amount, total, bound, skew):
    if amount == 2:
        one = jax.random.randint(own_key, (), max(1, total - bound), min(bound, total - 1) + 1)
        return jnp.stack([one, total - one])
    tallies = jnp.asarray(profile(amount, total, bound, skew), jnp.int32)
    pairs = (amount - 1) // 2
    giver, receiver = tallies[1:1 + 2 * pairs:2], tallies[2:2 + 2 * pairs:2]
    margin = jnp.minimum(giver - 1, bound - receiver)
    shifted = jax.random.randint(jax.random.fold_in(own_key, 1), (pairs,), 0, 1 << 20) % (margin + 1)
    tallies = tallies.at[1:1 + 2 * pairs:2].set(giver - shifted).at[2:2 + 2 * pairs:2].set(receiver + shifted)
    return tallies[jax.random.permutation(jax.random.fold_in(own_key, 2), amount)]


def scatter_about(rng, extent, width, most, shards=(), held_as=jnp.bfloat16):
    drawn = jax.random.normal(rng, extent, jnp.float32) * width
    if len(shards) > 0:
        drawn = level_of(rng, extent, shards, -0.22, 0.18) * drawn
    return jnp.clip(drawn, min=-most, max=most).astype(held_as)


def setup_inputs(seed: int = 0) -> dict:
    splits = jax.random.split(jax.random.key(seed), 14)
    return {
        "tokens": scatter_about(splits[0], (BATCH, SEQ, D), 1.0, 6.0, ((0, 16),)),
        "gain_attn": jnp.clip(1.0 + 0.1 * jax.random.normal(splits[1], (D,), jnp.float32), 0.5, 1.5),
        "query_key_value_weight": scatter_about(splits[2], (3, D, HEADS * HEAD_DIM), D ** -0.5, 0.21875, ((2, 2),)),
        "attn_out_weight": scatter_about(splits[3], (HEADS * HEAD_DIM, D), (HEADS * HEAD_DIM // 16) ** -0.5, 0.875, ((0, 2),)),
        "position_bias_matrix": scatter_about(splits[4], (BUCKETS, HEADS), 0.7, 4.0, ((1, 2),), jnp.float32),
        "gain_expert": jnp.clip(1.0 + 0.1 * jax.random.normal(splits[5], (D,), jnp.float32), 0.5, 1.5),
        "router": scatter_about(splits[6], (D, EXPERTS), D ** -0.5, 0.21875, (), jnp.float32),
        "expert_in": scatter_about(splits[7], (EXPERTS, D, FF), D ** -0.5, 0.21875, ((2, 2),)),
        "expert_out": scatter_about(splits[8], (EXPERTS, FF, D), (FF // 16) ** -0.5, 0.4375, ((1, 2),)),
        "segments": jax.vmap(lambda own: jnp.searchsorted(jnp.cumsum(ragged(own, 4, SEQ, SEQ // 2, 0)), jnp.arange(SEQ), side="right"))(jax.random.split(splits[9], BATCH)).reshape((BATCH, SEQ)).astype(jnp.int32),
        "routes": draw_routes(jax.random.fold_in(splits[13], 71), 0),
        "slots": draw_slots(jax.random.fold_in(splits[13], 71), 0),
        "cotangent": scatter_about(splits[12], (BATCH, SEQ, D), 1.0, 6.0, ((0, 16),)),
    }


EPS = 1e-06
NEG = -1e+30
HIGH = lax.Precision.HIGHEST

@jax.custom_vjp
def low(v):
    return lax.optimization_barrier(v.astype(jnp.bfloat16)).astype(jnp.float32)

@jax.custom_vjp
def low_back(v):
    return v

def low_keep(v):
    return (low(v), None)

def low_pass(kept, grad):
    return (grad,)

def back_keep(v):
    return (v, None)

def back_low(kept, grad):
    return (low(grad),)
low.defvjp(low_keep, low_pass)
low_back.defvjp(back_keep, back_low)

def relative_bucket_index(length):
    places = jnp.arange(length, dtype=jnp.int32)
    offset = places[None, :] - places[:, None]
    distance = jnp.abs(offset)
    coarse = jnp.full_like(distance, 8)
    for limit in (12, 16, 23, 32, 46, 64, 91):
        coarse = coarse + (distance >= limit).astype(jnp.int32)
    bucket = jnp.where(distance < 8, distance, coarse)
    return bucket + 16 * (offset > 0).astype(jnp.int32)

def row_norm(values, gain):
    return values * lax.rsqrt(lax.optimization_barrier(jnp.mean(values * values, axis=-1, keepdims=True)) + EPS) * gain

def matmul(left, right):
    return jnp.matmul(left, right, precision=HIGH)

def attend_one(bias_group, item):
    query, keys, values, segment = item
    raw = jnp.einsum('ihd,jhd->hij', query, keys, precision=HIGH) * HEAD_DIM ** (-0.5)
    same = segment[:, None] == segment[None, :]
    scores = jnp.where(same[None], low_back(raw) + bias_group, NEG)
    probs = low(jax.nn.softmax(scores, axis=-1))
    mixed = jnp.einsum('hij,jhd->ihd', probs, values, precision=HIGH)
    return low_back(low(mixed))

def layer(inputs, weights, bucket, segment_ids, route_ids, slot_ids):
    gain_a, qkv, out_a, table, gain_e, rout, w_first, w_second = weights
    count = SEQS_DEV * SEQ
    flat = inputs.reshape(count, D)
    act_a = low(row_norm(flat, gain_a))
    bias = jnp.transpose(table[bucket], (2, 0, 1))
    group_heads = HEADS // N_TENSOR
    group_width = group_heads * HEAD_DIM
    group_ff = FF // N_TENSOR
    attention = jnp.zeros((count, D), jnp.float32)
    for group in range(N_TENSOR):
        lower = group * group_width
        act_g = low_back(act_a)
        parts = []
        for index in range(3):
            made = matmul(act_g, qkv[index][:, lower:lower + group_width])
            parts.append(low_back(low(made)).reshape(SEQS_DEV, SEQ, group_heads, HEAD_DIM))
        bias_group = bias[group * group_heads:(group + 1) * group_heads]
        mixed = lax.map(jax.checkpoint(partial(attend_one, bias_group)), (parts[0], parts[1], parts[2], segment_ids))
        part = matmul(mixed.reshape(count, group_width), out_a[lower:lower + group_width, :])
        attention = attention + low_back(low(part))
    hidden = flat + attention
    expert_normed_input = row_norm(hidden, gain_e)
    chance = jax.nn.softmax(matmul(expert_normed_input, rout), axis=-1)
    route_flat = route_ids.reshape(count)
    gate = jnp.take_along_axis(chance, route_flat[:, None], axis=1)[:, 0]
    place = route_flat * CAP + slot_ids.reshape(count)
    act_e = low(expert_normed_input)
    moe = jnp.zeros((EXPERTS * CAP, D), jnp.float32)
    for group in range(N_TENSOR):
        lower = group * group_ff
        act_g = low_back(act_e)
        dispatched = jnp.zeros((EXPERTS * CAP, D), jnp.float32).at[place].set(act_g).reshape(EXPERTS, CAP, D)
        inner = low_back(jnp.einsum('ecd,edf->ecf', dispatched, w_first[:, :, lower:lower + group_ff], precision=HIGH))
        activated = low(jax.nn.gelu(inner))
        returned = jnp.einsum('ecf,efd->ecd', activated, w_second[:, lower:lower + group_ff, :], precision=HIGH)
        moe = moe + low_back(low(returned.reshape(EXPERTS * CAP, D)))
    result = hidden + moe[place] * gate[:, None]
    return result.reshape(SEQS_DEV, SEQ, D)

def reference(tokens, gain_attn, query_key_value_weight, attn_out_weight, position_bias_matrix, gain_expert, router, expert_in, expert_out, segments, routes, slots, cotangent):
    params = (gain_attn, query_key_value_weight.astype(jnp.float32), attn_out_weight.astype(jnp.float32), position_bias_matrix, gain_expert, router, expert_in.astype(jnp.float32), expert_out.astype(jnp.float32))
    blocks = BATCH // SEQS_DEV
    bucket = relative_bucket_index(SEQ)

    def split(array):
        return array.reshape((blocks, SEQS_DEV) + array.shape[1:])

    def step(totals, item):
        block_tokens, block_cot, block_seg, block_route, block_slot = item

        def forward(inputs, *weights):
            return layer(inputs, weights, bucket, block_seg, block_route, block_slot)
        result, pull = jax.vjp(forward, block_tokens.astype(jnp.float32), *params)
        grads = pull(block_cot.astype(jnp.float32))
        totals = tuple((a + b for a, b in zip(totals, grads[1:])))
        return (totals, (result.astype(jnp.bfloat16), grads[0]))
    init = tuple((jnp.zeros_like(value) for value in params))
    items = (split(tokens), split(cotangent), split(segments), split(routes), split(slots))
    totals, (results, grad_inputs) = lax.scan(step, init, items)
    return (results.reshape(tokens.shape), grad_inputs.reshape(tokens.shape), totals[0], totals[1], totals[2], totals[3], totals[4], totals[5], totals[6], totals[7])
```

```python
import functools

import jax
import jax.numpy as jnp
from jax import lax
from jax.experimental import pallas as pl
from jax.experimental.pallas import tpu as pltpu
from jax.sharding import PartitionSpec as P

HEAD_DIM = 64
CAP = 320
EPS = 1e-06
NEG = -1e30
HIGH = lax.Precision.HIGHEST
BLOCK = 128
LIMIT = 48 * 1024 * 1024
F32 = jnp.float32
BF16 = jnp.bfloat16


def band_bucket():
    row = lax.broadcasted_iota(jnp.int32, (BLOCK, 5 * BLOCK), 0)
    column = lax.broadcasted_iota(jnp.int32, (BLOCK, 5 * BLOCK), 1)
    offset = column - 2 * BLOCK - row
    distance = jnp.abs(offset)
    coarse = jnp.full_like(distance, 8)
    for limit in (12, 16, 23, 32, 46, 64, 91):
        coarse = coarse + (distance >= limit).astype(jnp.int32)
    bucket = jnp.where(distance < 8, distance, coarse)
    return bucket + 16 * (offset > 0).astype(jnp.int32)


def band_bias(table, bucket):
    result = jnp.zeros((table.shape[1],) + bucket.shape, F32)
    for index in range(table.shape[0]):
        result = jnp.where(bucket[None] == index, table[index][:, None, None], result)
    return result


def band_table_grad(band, bucket, count):
    rows = [
        jnp.sum(jnp.where(bucket[None] == index, band, 0.0), axis=(1, 2)) for index in range(count)
    ]
    return jnp.stack(rows)


def row_norm(values, gain):
    inverse = lax.rsqrt(jnp.mean(values * values, axis=-1, keepdims=True) + EPS)
    return (values * inverse * gain, inverse)


def norm_back(grad_out, values, inverse, gain):
    scaled = grad_out * gain
    grad_gain = jnp.sum(grad_out * values * inverse, axis=0)
    grad_in = inverse * scaled - values * inverse**3 * jnp.mean(
        scaled * values, axis=-1, keepdims=True
    )
    return (grad_in, grad_gain)


def dot_t(left, right):
    return lax.dot_general(left, right, (((1,), (1,)), ((), ())), preferred_element_type=F32)


def dot_n(left, right):
    return lax.dot_general(left, right, (((1,), (0,)), ((), ())), preferred_element_type=F32)


def t_dot(left, right):
    return lax.dot_general(left, right, (((0,), (0,)), ((), ())), preferred_element_type=F32)


def bias_row(bias_ref, head, place, tiles):
    parts = []
    for tile in range(tiles):
        start = (jnp.clip(tile - place, -2, 2) + 2) * BLOCK
        parts.append(bias_ref[head, :, pl.ds(pl.multiple_of(start, BLOCK), BLOCK)])
    return jnp.concatenate(parts, axis=1)


def lane_half(array, head):
    lane = lax.broadcasted_iota(jnp.int32, array.shape, 1)
    return jnp.where((lane >= HEAD_DIM) == (head == 1), array, jnp.zeros_like(array))


def attend_kernel(q_ref, k_ref, v_ref, bias_ref, seg_col_ref, seg_row_ref, out_ref):
    place = pl.program_id(1)
    tiles = k_ref.shape[1] // BLOCK
    query, keys, values = q_ref[0], k_ref[0], v_ref[0]
    same = seg_col_ref[...] == seg_row_ref[...]
    total = None
    for head in range(2):
        raw = dot_t(lane_half(query, head), keys) * (HEAD_DIM**-0.5)
        scores = jnp.where(same, raw + bias_row(bias_ref, head, place, tiles), NEG)
        expo = jnp.exp(scores - jnp.max(scores, axis=-1, keepdims=True))
        probs = expo * (1.0 / jnp.sum(expo, axis=-1, keepdims=True))
        mixed = lane_half(dot_n(probs.astype(BF16), values), head)
        total = mixed if total is None else total + mixed
    out_ref[...] = total.astype(BF16)


def attend_back_kernel(
    q_ref, k_ref, v_ref, bias_ref, seg_col_ref, seg_row_ref, grad_ref, out_ref, band_ref, dk_ref, dv_ref
):
    place = pl.program_id(1)
    tiles = k_ref.shape[1] // BLOCK
    scale = HEAD_DIM**-0.5

    @pl.when(place == 0)
    def _():
        dk_ref[...] = jnp.zeros_like(dk_ref)
        dv_ref[...] = jnp.zeros_like(dv_ref)
        band_ref[...] = jnp.zeros_like(band_ref)

    query, keys, values, grad = q_ref[0], k_ref[0], v_ref[0], grad_ref[...]
    same = seg_col_ref[...] == seg_row_ref[...]
    dq = None
    for head in range(2):
        query_h, grad_h = lane_half(query, head), lane_half(grad, head)
        raw = dot_t(query_h, keys) * scale
        scores = jnp.where(same, raw + bias_row(bias_ref, head, place, tiles), NEG)
        expo = jnp.exp(scores - jnp.max(scores, axis=-1, keepdims=True))
        probs = expo * (1.0 / jnp.sum(expo, axis=-1, keepdims=True))
        grad_probs = dot_t(grad_h, values)
        inner = jnp.sum(grad_probs * probs, axis=-1, keepdims=True)
        grad_scores = probs * (grad_probs - inner)
        for tile in range(tiles):
            start = (jnp.clip(tile - place, -2, 2) + 2) * BLOCK
            band_ref[head, :, pl.ds(pl.multiple_of(start, BLOCK), BLOCK)] += grad_scores[
                :, tile * BLOCK : (tile + 1) * BLOCK
            ]
        low = grad_scores.astype(BF16)
        dv_ref[...] += t_dot(probs.astype(BF16), grad_h)
        dk_ref[...] += t_dot(low, query_h)
        part = lane_half(dot_n(low, keys), head)
        dq = part if dq is None else dq + part
    rows = pl.ds(pl.multiple_of(place * BLOCK, BLOCK), BLOCK)
    out_ref[0, rows, :] = (dq * scale).astype(BF16)

    @pl.when(place == tiles - 1)
    def _():
        out_ref[1] = (dk_ref[...] * scale).astype(BF16)
        out_ref[2] = dv_ref[...].astype(BF16)


def attention_specs(length):
    return [
        pl.BlockSpec((1, BLOCK, BLOCK), lambda p, i: (0, i, p)),
        pl.BlockSpec((1, length, BLOCK), lambda p, i: (1, 0, p)),
        pl.BlockSpec((1, length, BLOCK), lambda p, i: (2, 0, p)),
        pl.BlockSpec((2, BLOCK, 5 * BLOCK), lambda p, i: (p, 0, 0)),
        pl.BlockSpec((BLOCK, 1), lambda p, i: (i, 0)),
        pl.BlockSpec((1, length), lambda p, i: (0, 0)),
    ]


def attend(projected, bias, segment):
    _, length, width = projected.shape
    pairs = width // BLOCK
    return pl.pallas_call(
        attend_kernel,
        grid=(pairs, length // BLOCK),
        in_specs=attention_specs(length),
        out_specs=pl.BlockSpec((BLOCK, BLOCK), lambda p, i: (i, p)),
        out_shape=jax.ShapeDtypeStruct((length, width), BF16),
        compiler_params=pltpu.CompilerParams(vmem_limit_bytes=LIMIT),
        cost_estimate=pl.CostEstimate(
            flops=16 * length * length * width, bytes_accessed=8 * length * width, transcendentals=6 * length * length
        ),
    )(projected, projected, projected, bias, segment[:, None], segment[None, :])


def attend_back(projected, bias, segment, grad):
    _, length, width = projected.shape
    pairs = width // BLOCK
    return pl.pallas_call(
        attend_back_kernel,
        grid=(pairs, length // BLOCK),
        in_specs=attention_specs(length) + [pl.BlockSpec((BLOCK, BLOCK), lambda p, i: (i, p))],
        out_specs=[
            pl.BlockSpec((3, length, BLOCK), lambda p, i: (0, 0, p)),
            pl.BlockSpec((2, BLOCK, 5 * BLOCK), lambda p, i: (p, 0, 0)),
        ],
        out_shape=[
            jax.ShapeDtypeStruct((3, length, width), BF16),
            jax.ShapeDtypeStruct((2 * pairs, BLOCK, 5 * BLOCK), F32),
        ],
        scratch_shapes=[pltpu.VMEM((length, BLOCK), F32), pltpu.VMEM((length, BLOCK), F32)],
        compiler_params=pltpu.CompilerParams(vmem_limit_bytes=LIMIT),
        cost_estimate=pl.CostEstimate(
            flops=48 * length * length * width, bytes_accessed=16 * length * width, transcendentals=6 * length * length
        ),
    )(projected, projected, projected, bias, segment[:, None], segment[None, :], grad)


def pair_sum(part, size):
    if size != 2:
        return lax.psum(part.astype(F32), "tensor")
    other = lax.ppermute(part, "tensor", [(0, 1), (1, 0)])
    return part.astype(F32) + other.astype(F32)


def bits_of(size):
    bits = size.bit_length() - 1
    assert 1 << bits == size
    return bits


def swap(array, size, bit):
    return lax.ppermute(array, "dp", [(i, i ^ (1 << bit)) for i in range(size)])


def scatter_sum(unit, size, order):
    bits = bits_of(size)
    rows, columns = unit.shape
    me = lax.axis_index("dp")
    held = unit.reshape((2,) * bits + (rows // size, columns))
    left = list(range(bits - 1, -1, -1))
    for step, bit in enumerate(order):
        axis = left.index(bit)
        mine = (me >> bit) & 1
        sent = lax.dynamic_index_in_dim(held, 1 - mine, axis, keepdims=False)
        kept = lax.dynamic_index_in_dim(held, mine, axis, keepdims=False)
        got = swap(sent, size, bit)
        held = kept.astype(F32) + got.astype(F32)
        if step < bits - 1:
            held = held.astype(BF16)
        left.remove(bit)
    return held


def small_sum(array, size):
    for bit in range(bits_of(size)):
        array = array + swap(array, size, bit)
    return array


def orders_of(size):
    bits = bits_of(size)
    if bits == 4:
        return [(0, 1, 2, 3), (1, 0, 2, 3), (2, 0, 1, 3)]
    return [tuple(range(bits)), tuple(range(bits - 1, -1, -1)), tuple(range(bits))]


def body(
    dp,
    tp,
    tokens,
    gain_attn,
    query_key_value_weight,
    attn_out_weight,
    position_bias_matrix,
    gain_expert,
    router,
    expert_in,
    expert_out,
    segments,
    routes,
    slots,
    cotangent,
):
    seqs, length, width = tokens.shape
    count = seqs * length
    experts = expert_in.shape[0]
    places = experts * CAP
    local = attn_out_weight.shape[0]
    orders = orders_of(dp)
    inputs = tokens.astype(F32).reshape(count, width)
    normed_a, inverse_a = row_norm(inputs, gain_attn)
    act_a = normed_a.astype(BF16)
    projected = jnp.einsum(
        "td,cde->cte", act_a, query_key_value_weight, preferred_element_type=F32
    ).astype(BF16)
    bucket = band_bucket()
    bias = band_bias(position_bias_matrix, bucket)
    per_seq = projected.reshape(3, seqs, length, local)
    flat_att = jnp.concatenate([attend(per_seq[:, s], bias, segments[s]) for s in range(seqs)], axis=0)
    attn_part = jnp.dot(flat_att, attn_out_weight, preferred_element_type=F32).astype(BF16)
    hidden_res = inputs + pair_sum(attn_part, tp)
    normed_e, inverse_e = row_norm(hidden_res, gain_expert)
    logits = jnp.dot(normed_e, router, precision=HIGH, preferred_element_type=F32)
    chance = jax.nn.softmax(logits, axis=-1)
    route_flat = routes.reshape(count)
    onehot = (route_flat[:, None] == jnp.arange(experts, dtype=jnp.int32)[None, :]).astype(F32)
    gate = jnp.sum(chance * onehot, axis=-1)
    block = jnp.arange(count, dtype=jnp.int32) // length
    place = (block * places) + route_flat * CAP + slots.reshape(count)
    spot = jnp.arange(seqs * places, dtype=jnp.int32)
    to_slot = (spot[:, None] == place[None, :]).astype(BF16)
    to_token = (place[:, None] == spot[None, :]).astype(BF16)
    act_e = normed_e.astype(BF16)
    upstream = cotangent.astype(F32).reshape(count, width)
    scaled_up = (upstream * gate[:, None]).astype(BF16)

    def dispatch(array):
        made = jnp.dot(to_slot, array, preferred_element_type=F32).astype(BF16)
        made = made.reshape(seqs, experts, CAP, width)
        return jnp.transpose(made, (1, 0, 2, 3)).reshape(experts, seqs * CAP, width)

    def collect(array):
        array = jnp.transpose(array.reshape(experts, seqs, CAP, width), (1, 0, 2, 3))
        array = array.reshape(seqs * places, width)
        return jnp.dot(to_token, array, preferred_element_type=F32).astype(BF16)

    dispatched = dispatch(act_e)
    slot_grad = dispatch(scaled_up)
    inner = jnp.einsum("ecd,edf->ecf", dispatched, expert_in, preferred_element_type=F32)
    activated = jax.nn.gelu(inner).astype(BF16)
    grad_out_t = [
        jnp.einsum("cd,cf->df", slot_grad[e], activated[e], preferred_element_type=F32).astype(BF16)
        for e in range(experts)
    ]
    summed_out = [scatter_sum(g, dp, orders[e % 2]) for e, g in enumerate(grad_out_t)]
    grad_act = jnp.einsum("ecd,efd->ecf", slot_grad, expert_out, preferred_element_type=F32)
    unused, gelu_pull = jax.vjp(jax.nn.gelu, inner)
    grad_inner = gelu_pull(grad_act)[0].astype(BF16)
    grad_in = [
        jnp.einsum("cd,cf->df", dispatched[e], grad_inner[e], preferred_element_type=F32).astype(BF16)
        for e in range(experts)
    ]
    summed_in = [scatter_sum(g, dp, orders[(2, 0, 1, 2)[e % 4]]) for e, g in enumerate(grad_in)]
    returned = jnp.einsum("ecf,efd->ecd", activated, expert_out, preferred_element_type=F32).astype(BF16)
    expert_total = pair_sum(collect(returned), tp)
    grad_disp = jnp.einsum("ecf,edf->ecd", grad_inner, expert_in, preferred_element_type=F32).astype(BF16)
    back_expert = pair_sum(collect(grad_disp), tp)
    output = (hidden_res + expert_total * gate[:, None]).astype(BF16).reshape(seqs, length, width)
    grad_gate = jnp.sum(upstream * expert_total, axis=-1)
    grad_logits = (grad_gate * gate)[:, None] * (onehot - chance)
    grad_router = jnp.dot(normed_e.T, grad_logits, precision=HIGH, preferred_element_type=F32)
    grad_normed_e = back_expert + jnp.dot(
        grad_logits, router.T, precision=HIGH, preferred_element_type=F32
    )
    grad_hidden_part, grad_gain_expert = norm_back(grad_normed_e, hidden_res, inverse_e, gain_expert)
    grad_hidden = upstream + grad_hidden_part
    grad_hidden_low = grad_hidden.astype(BF16)
    grad_attn_out_t = jnp.dot(grad_hidden_low.T, flat_att, preferred_element_type=F32).astype(BF16)
    grad_attended = jnp.dot(
        grad_hidden_low, attn_out_weight.T, preferred_element_type=F32
    ).astype(BF16)
    parts, bands = [], None
    for s in range(seqs):
        part, band = attend_back(
            per_seq[:, s], bias, segments[s], grad_attended.reshape(seqs, length, local)[s]
        )
        parts.append(part)
        bands = band if bands is None else bands + band
    grads = jnp.concatenate(parts, axis=1)
    weight_grads = [
        jnp.dot(act_a.T, grads[k], preferred_element_type=F32).astype(BF16) for k in range(3)
    ]
    last = scatter_sum(jnp.concatenate(weight_grads + [grad_attn_out_t], axis=1), dp, orders[0])
    grad_act_a = jnp.einsum("cte,cde->td", grads, query_key_value_weight, preferred_element_type=F32)
    grad_table = band_table_grad(bands, bucket, position_bias_matrix.shape[0])
    back_attn = pair_sum(grad_act_a.astype(BF16), tp)
    grad_in_part, grad_gain_attn = norm_back(back_attn, inputs, inverse_a, gain_attn)
    grad_tokens = (grad_hidden + grad_in_part).reshape(seqs, length, width)
    small = jnp.concatenate(
        [grad_gain_attn, grad_gain_expert, grad_router.T.reshape(-1), grad_table.reshape(-1)]
    )
    small = small_sum(small, dp)
    me = lax.axis_index("dp")
    share = width // dp
    wide = lax.dynamic_slice_in_dim(small[: 6 * width].reshape(6, width), me * share, share, axis=1)
    return (
        output,
        grad_tokens,
        wide[0],
        jnp.transpose(last[:, : 3 * local].reshape(share, 3, local), (1, 0, 2)),
        last[:, 3 * local :].T,
        small[6 * width :].reshape(position_bias_matrix.shape),
        wide[1],
        wide[2:].T,
        jnp.stack(summed_in),
        jnp.transpose(jnp.stack(summed_out), (0, 2, 1)),
    )


def solution(mesh):
    in_specs = (
        P("dp", None, None),
        P(),
        P(None, None, "tensor"),
        P("tensor", None),
        P(None, "tensor"),
        P(),
        P(),
        P(None, None, "tensor"),
        P(None, "tensor", None),
        P("dp", None),
        P("dp", None),
        P("dp", None),
        P("dp", None, None),
    )
    out_specs = (
        P("dp", None, None),
        P("dp", None, None),
        P("dp"),
        P(None, "dp", "tensor"),
        P("tensor", "dp"),
        P(None, "tensor"),
        P("dp"),
        P("dp", None),
        P(None, "dp", "tensor"),
        P(None, "tensor", "dp"),
    )
    run = functools.partial(body, mesh.shape["dp"], mesh.shape["tensor"])
    return jax.shard_map(run, mesh=mesh, in_specs=in_specs, out_specs=out_specs, check_vma=False)
```

```python
import functools

import jax
import jax.numpy as jnp
from jax import lax
from jax.experimental import pallas as pl
from jax.experimental.pallas import tpu as pltpu
from jax.sharding import PartitionSpec as P

HEAD_DIM = 64
CAP = 320
EPS = 1e-06
NEG = -1e30
HIGH = lax.Precision.HIGHEST
BLOCK = 128
SPAN = 6 * BLOCK
LIMIT = 48 * 1024 * 1024
F32 = jnp.float32
BF16 = jnp.bfloat16


def offset_bucket():
    lane = jnp.arange(SPAN, dtype=jnp.int32)
    offset = jnp.where(lane < 5 * BLOCK, lane, lane - SPAN) - 2 * BLOCK
    distance = jnp.abs(offset)
    coarse = jnp.full_like(distance, 8)
    for limit in (12, 16, 23, 32, 46, 64, 91):
        coarse = coarse + (distance >= limit).astype(jnp.int32)
    bucket = jnp.where(distance < 8, distance, coarse)
    return bucket + 16 * (offset > 0).astype(jnp.int32)


def offset_bias(table, bucket):
    result = jnp.zeros((table.shape[1], SPAN), F32)
    for index in range(table.shape[0]):
        result = jnp.where(bucket[None] == index, table[index][:, None], result)
    return result.reshape(-1, 2, SPAN)


def offset_table_grad(sums, bucket, count):
    flat = sums.reshape(-1, SPAN)
    same = bucket[None, :] == jnp.arange(count, dtype=jnp.int32)[:, None]
    return jnp.sum(jnp.where(same[:, None, :], flat[None], 0.0), axis=-1)


def tile_ranges(segment):
    rows = segment.reshape(-1, BLOCK)
    first = jnp.sum((segment[None] < rows[:, :1]).astype(jnp.int32), axis=1) // BLOCK
    end = (jnp.sum((segment[None] <= rows[:, -1:]).astype(jnp.int32), axis=1) + BLOCK - 1) // BLOCK
    return jnp.concatenate([first, end])


def row_norm(values, gain):
    inverse = lax.rsqrt(jnp.mean(values * values, axis=-1, keepdims=True) + EPS)
    return (values * inverse * gain, inverse)


def norm_back(grad_out, values, inverse, gain):
    scaled = grad_out * gain
    grad_gain = jnp.sum(grad_out * values * inverse, axis=0)
    grad_in = inverse * scaled - values * inverse**3 * jnp.mean(
        scaled * values, axis=-1, keepdims=True
    )
    return (grad_in, grad_gain)


def dot_t(left, right):
    return lax.dot_general(left, right, (((1,), (1,)), ((), ())), preferred_element_type=F32)


def dot_n(left, right):
    return lax.dot_general(left, right, (((1,), (0,)), ((), ())), preferred_element_type=F32)


def t_dot(left, right):
    return lax.dot_general(left, right, (((0,), (0,)), ((), ())), preferred_element_type=F32)


def skew_rows(vector):
    made = jnp.broadcast_to(vector, (8, SPAN))
    row = lax.broadcasted_iota(jnp.int32, (8, SPAN), 0)
    for step in (1, 2, 4):
        made = jnp.where((row & step) != 0, pltpu.roll(made, step, 1), made)
    for step in (8, 16, 32, 64):
        made = jnp.concatenate([made, pltpu.roll(made, step, 1)], axis=0)
    return made


def unskew_sum(band):
    held = jnp.concatenate([band, jnp.zeros((BLOCK, SPAN - band.shape[1]), F32)], axis=1)
    for step in (64, 32, 16, 8):
        held = held[:step] + pltpu.roll(held[step:], SPAN - step, 1)
    row = lax.broadcasted_iota(jnp.int32, (8, SPAN), 0)
    for step in (1, 2, 4):
        held = jnp.where((row & step) != 0, pltpu.roll(held, SPAN - step, 1), held)
    return jnp.sum(held, axis=0, keepdims=True)


def band_lanes(tile, place):
    start = (jnp.clip(tile - place, -2, 2) + 2) * BLOCK
    return pl.ds(pl.multiple_of(start, BLOCK), BLOCK)


def lane_half(array, head):
    lane = lax.broadcasted_iota(jnp.int32, array.shape, 1)
    return jnp.where((lane >= HEAD_DIM) == (head == 1), array, jnp.zeros_like(array))


def over_windows(range_ref, place, tiles, step):
    first, end = range_ref[place], range_ref[tiles + place]
    need = end - first
    sizes = sorted({min(3, tiles), min(5, tiles), tiles})
    below = 0
    for size in sizes:

        @pl.when((need > below) & (need <= size))
        def _(size=size):
            step(jnp.minimum(first, tiles - size), size)

        below = size


def window_scores(query_h, keys, same, bias_ref, head, place, start, size):
    raw = dot_t(query_h, keys)
    bias = jnp.concatenate(
        [bias_ref[head, :, band_lanes(start + tile, place)] for tile in range(size)], axis=1
    )
    return jnp.where(same, raw + bias, NEG)


def attend_kernel(range_ref, q_ref, k_ref, v_ref, vec_ref, seg_col_ref, seg_row_ref, out_ref, bias_ref):
    place = pl.program_id(1)
    tiles = k_ref.shape[1] // BLOCK

    @pl.when(place == 0)
    def _():
        for head in range(2):
            bias_ref[head] = skew_rows(vec_ref[0, head : head + 1, :])[:, : 5 * BLOCK]

    def step(start, size):
        window = pl.ds(pl.multiple_of(start * BLOCK, BLOCK), size * BLOCK)
        query = q_ref[0] * jnp.asarray(HEAD_DIM**-0.5, BF16)
        keys, values = k_ref[0, window, :], v_ref[0, window, :]
        same = seg_col_ref[...] == seg_row_ref[:, window]
        total = None
        for head in range(2):
            scores = window_scores(
                lane_half(query, head), keys, same, bias_ref, head, place, start, size
            )
            expo = jnp.exp(scores - jnp.max(scores, axis=-1, keepdims=True))
            inverse = 1.0 / jnp.sum(expo, axis=-1, keepdims=True)
            mixed = lane_half(dot_n(expo.astype(BF16), values) * inverse, head)
            total = mixed if total is None else total + mixed
        out_ref[...] = total.astype(BF16)

    over_windows(range_ref, place, tiles, step)


def attend_back_kernel(
    range_ref,
    q_ref,
    k_ref,
    v_ref,
    vec_ref,
    seg_col_ref,
    seg_row_ref,
    grad_ref,
    out_ref,
    sums_ref,
    bias_ref,
    band_ref,
    dk_ref,
    dv_ref,
):
    place = pl.program_id(1)
    tiles = k_ref.shape[1] // BLOCK

    @pl.when(place == 0)
    def _():
        dk_ref[...] = jnp.zeros_like(dk_ref)
        dv_ref[...] = jnp.zeros_like(dv_ref)
        band_ref[...] = jnp.zeros_like(band_ref)
        for head in range(2):
            bias_ref[head] = skew_rows(vec_ref[0, head : head + 1, :])[:, : 5 * BLOCK]

    rows = pl.ds(pl.multiple_of(place * BLOCK, BLOCK), BLOCK)

    def step(start, size):
        window = pl.ds(pl.multiple_of(start * BLOCK, BLOCK), size * BLOCK)
        query = q_ref[0] * jnp.asarray(HEAD_DIM**-0.5, BF16)
        keys, values, grad = k_ref[0, window, :], v_ref[0, window, :], grad_ref[...]
        same = seg_col_ref[...] == seg_row_ref[:, window]
        dq = None
        for head in range(2):
            query_h, grad_h = lane_half(query, head), lane_half(grad, head)
            scores = window_scores(query_h, keys, same, bias_ref, head, place, start, size)
            expo = jnp.exp(scores - jnp.max(scores, axis=-1, keepdims=True))
            probs = expo * (1.0 / jnp.sum(expo, axis=-1, keepdims=True))
            grad_probs = dot_t(grad_h, values)
            inner = jnp.sum(grad_probs * probs, axis=-1, keepdims=True)
            grad_scores = probs * (grad_probs - inner)
            for tile in range(size):
                band_ref[head, :, band_lanes(start + tile, place)] += grad_scores[
                    :, tile * BLOCK : (tile + 1) * BLOCK
                ]
            low = grad_scores.astype(BF16)
            dv_ref[window, :] += t_dot(probs.astype(BF16), grad_h)
            dk_ref[window, :] += t_dot(low, query_h)
            part = lane_half(dot_n(low, keys), head)
            dq = part if dq is None else dq + part
        out_ref[0, rows, :] = (dq * HEAD_DIM**-0.5).astype(BF16)

    over_windows(range_ref, place, tiles, step)

    @pl.when(place == tiles - 1)
    def _():
        out_ref[1] = dk_ref[...].astype(BF16)
        out_ref[2] = dv_ref[...].astype(BF16)
        for head in range(2):
            sums_ref[0, head : head + 1, :] = unskew_sum(band_ref[head])


def attention_specs(length):
    return [
        pl.BlockSpec((1, BLOCK, BLOCK), lambda p, i, r: (0, i, p)),
        pl.BlockSpec((1, length, BLOCK), lambda p, i, r: (1, 0, p)),
        pl.BlockSpec((1, length, BLOCK), lambda p, i, r: (2, 0, p)),
        pl.BlockSpec((1, 2, SPAN), lambda p, i, r: (p, 0, 0)),
        pl.BlockSpec((BLOCK, 1), lambda p, i, r: (i, 0)),
        pl.BlockSpec((1, length), lambda p, i, r: (0, 0)),
    ]


def attend(projected, bias, segment):
    _, length, width = projected.shape
    pairs = width // BLOCK
    return pl.pallas_call(
        attend_kernel,
        grid_spec=pltpu.PrefetchScalarGridSpec(
            num_scalar_prefetch=1,
            grid=(pairs, length // BLOCK),
            in_specs=attention_specs(length),
            out_specs=pl.BlockSpec((BLOCK, BLOCK), lambda p, i, r: (i, p)),
            scratch_shapes=[pltpu.VMEM((2, BLOCK, 5 * BLOCK), F32)],
        ),
        out_shape=jax.ShapeDtypeStruct((length, width), BF16),
        compiler_params=pltpu.CompilerParams(vmem_limit_bytes=LIMIT),
        cost_estimate=pl.CostEstimate(
            flops=16 * length * length * width, bytes_accessed=8 * length * width, transcendentals=6 * length * length
        ),
    )(tile_ranges(segment), projected, projected, projected, bias, segment[:, None], segment[None, :])


def attend_back(projected, bias, segment, grad):
    _, length, width = projected.shape
    pairs = width // BLOCK
    return pl.pallas_call(
        attend_back_kernel,
        grid_spec=pltpu.PrefetchScalarGridSpec(
            num_scalar_prefetch=1,
            grid=(pairs, length // BLOCK),
            in_specs=attention_specs(length) + [pl.BlockSpec((BLOCK, BLOCK), lambda p, i, r: (i, p))],
            out_specs=[
                pl.BlockSpec((3, length, BLOCK), lambda p, i, r: (0, 0, p)),
                pl.BlockSpec((1, 2, SPAN), lambda p, i, r: (p, 0, 0)),
            ],
            scratch_shapes=[
                pltpu.VMEM((2, BLOCK, 5 * BLOCK), F32),
                pltpu.VMEM((2, BLOCK, 5 * BLOCK), F32),
                pltpu.VMEM((length, BLOCK), F32),
                pltpu.VMEM((length, BLOCK), F32),
            ],
        ),
        out_shape=[
            jax.ShapeDtypeStruct((3, length, width), BF16),
            jax.ShapeDtypeStruct((pairs, 2, SPAN), F32),
        ],
        compiler_params=pltpu.CompilerParams(vmem_limit_bytes=LIMIT),
        cost_estimate=pl.CostEstimate(
            flops=48 * length * length * width, bytes_accessed=16 * length * width, transcendentals=6 * length * length
        ),
    )(tile_ranges(segment), projected, projected, projected, bias, segment[:, None], segment[None, :], grad)


def pair_sum(part, size):
    if size != 2:
        return lax.psum(part.astype(F32), "tensor")
    other = lax.ppermute(part, "tensor", [(0, 1), (1, 0)])
    return part.astype(F32) + other.astype(F32)


def bits_of(size):
    bits = size.bit_length() - 1
    assert 1 << bits == size
    return bits


def swap(array, size, bit):
    return lax.ppermute(array, "dp", [(i, i ^ (1 << bit)) for i in range(size)])


def scatter_sum(unit, size, order):
    bits = bits_of(size)
    parts, rows, columns = unit.shape
    me = lax.axis_index("dp")
    held = unit.reshape((parts,) + (2,) * bits + (rows // size, columns))
    left = list(range(bits - 1, -1, -1))
    for step, bit in enumerate(order):
        axis = 1 + left.index(bit)
        mine = (me >> bit) & 1
        sent = lax.dynamic_index_in_dim(held, 1 - mine, axis, keepdims=False)
        kept = lax.dynamic_index_in_dim(held, mine, axis, keepdims=False)
        got = swap(sent, size, bit)
        held = kept.astype(F32) + got.astype(F32)
        if step < bits - 1:
            held = held.astype(BF16)
        left.remove(bit)
    return held


def small_sum(array, size):
    for bit in range(bits_of(size)):
        array = array + swap(array, size, bit)
    return array


def orders_of(size):
    bits = bits_of(size)
    if bits == 4:
        return [(0, 1, 2, 3), (1, 0, 2, 3)]
    return [tuple(range(bits)), tuple(range(bits - 1, -1, -1))]


def halves_sum(left, right, size):
    one, other = orders_of(size)
    return jnp.concatenate([scatter_sum(left, size, one), scatter_sum(right, size, other)], axis=0)


def body(
    dp,
    tp,
    tokens,
    gain_attn,
    query_key_value_weight,
    attn_out_weight,
    position_bias_matrix,
    gain_expert,
    router,
    expert_in,
    expert_out,
    segments,
    routes,
    slots,
    cotangent,
):
    seqs, length, width = tokens.shape
    count = seqs * length
    experts = expert_in.shape[0]
    places = experts * CAP
    local = attn_out_weight.shape[0]
    half = experts // 2
    inputs = tokens.astype(F32).reshape(count, width)
    normed_a, inverse_a = row_norm(inputs, gain_attn)
    act_a = normed_a.astype(BF16)
    projected = jnp.einsum(
        "td,cde->cte", act_a, query_key_value_weight, preferred_element_type=F32
    ).astype(BF16)
    bucket = offset_bucket()
    bias = offset_bias(position_bias_matrix, bucket)
    per_seq = projected.reshape(3, seqs, length, local)
    flat_att = jnp.concatenate([attend(per_seq[:, s], bias, segments[s]) for s in range(seqs)], axis=0)
    attn_part = jnp.dot(flat_att, attn_out_weight, preferred_element_type=F32).astype(BF16)
    hidden_res = inputs + pair_sum(attn_part, tp)
    normed_e, inverse_e = row_norm(hidden_res, gain_expert)
    logits = jnp.dot(normed_e, router, precision=HIGH, preferred_element_type=F32)
    chance = jax.nn.softmax(logits, axis=-1)
    route_flat = routes.reshape(count)
    onehot = (route_flat[:, None] == jnp.arange(experts, dtype=jnp.int32)[None, :]).astype(F32)
    gate = jnp.sum(chance * onehot, axis=-1)
    block = jnp.arange(count, dtype=jnp.int32) // length
    place = (block * places) + route_flat * CAP + slots.reshape(count)
    spot = jnp.arange(seqs * places, dtype=jnp.int32)
    to_slot = (spot[:, None] == place[None, :]).astype(BF16)
    to_token = (place[:, None] == spot[None, :]).astype(BF16)
    act_e = normed_e.astype(BF16)
    upstream = cotangent.astype(F32).reshape(count, width)
    scaled_up = (upstream * gate[:, None]).astype(BF16)

    def dispatch(array):
        made = jnp.dot(to_slot, array, preferred_element_type=F32).astype(BF16)
        made = made.reshape(seqs, experts, CAP, width)
        return jnp.transpose(made, (1, 0, 2, 3)).reshape(experts, seqs * CAP, width)

    def collect(array):
        array = jnp.transpose(array.reshape(experts, seqs, CAP, width), (1, 0, 2, 3))
        array = array.reshape(seqs * places, width)
        return jnp.dot(to_token, array, preferred_element_type=F32).astype(BF16)

    dispatched = dispatch(act_e)
    slot_grad = dispatch(scaled_up)
    inner = jnp.einsum("ecd,edf->ecf", dispatched, expert_in, preferred_element_type=F32)
    activated = jax.nn.gelu(inner).astype(BF16)
    pieces = (slice(0, half), slice(half, experts))
    grad_out_t = [
        jnp.einsum("ecd,ecf->edf", slot_grad[p], activated[p], preferred_element_type=F32).astype(BF16)
        for p in pieces
    ]
    grad_out_t, slot_grad = lax.optimization_barrier((grad_out_t, slot_grad))
    summed_out = halves_sum(*grad_out_t, dp)
    grad_act = jnp.einsum("ecd,efd->ecf", slot_grad, expert_out, preferred_element_type=F32)
    unused, gelu_pull = jax.vjp(jax.nn.gelu, inner)
    grad_inner = gelu_pull(grad_act)[0].astype(BF16)
    grad_in = [
        jnp.einsum("ecd,ecf->edf", dispatched[p], grad_inner[p], preferred_element_type=F32).astype(BF16)
        for p in pieces
    ]
    grad_in, activated, grad_inner = lax.optimization_barrier((grad_in, activated, grad_inner))
    summed_in = halves_sum(*grad_in, dp)
    returned = jnp.einsum("ecf,efd->ecd", activated, expert_out, preferred_element_type=F32).astype(BF16)
    expert_total = pair_sum(collect(returned), tp)
    grad_disp = jnp.einsum("ecf,edf->ecd", grad_inner, expert_in, preferred_element_type=F32).astype(BF16)
    back_expert = pair_sum(collect(grad_disp), tp)
    output = (hidden_res + expert_total * gate[:, None]).astype(BF16).reshape(seqs, length, width)
    grad_gate = jnp.sum(upstream * expert_total, axis=-1)
    grad_logits = (grad_gate * gate)[:, None] * (onehot - chance)
    grad_router = jnp.dot(normed_e.T, grad_logits, precision=HIGH, preferred_element_type=F32)
    grad_normed_e = back_expert + jnp.dot(
        grad_logits, router.T, precision=HIGH, preferred_element_type=F32
    )
    grad_hidden_part, grad_gain_expert = norm_back(grad_normed_e, hidden_res, inverse_e, gain_expert)
    grad_hidden = upstream + grad_hidden_part
    grad_hidden_low = grad_hidden.astype(BF16)
    grad_attn_out_t = jnp.dot(grad_hidden_low.T, flat_att, preferred_element_type=F32).astype(BF16)
    grad_attended = jnp.dot(
        grad_hidden_low, attn_out_weight.T, preferred_element_type=F32
    ).astype(BF16)
    parts, bands = [], None
    for s in range(seqs):
        part, band = attend_back(
            per_seq[:, s], bias, segments[s], grad_attended.reshape(seqs, length, local)[s]
        )
        parts.append(part)
        bands = band if bands is None else bands + band
    grads = jnp.concatenate(parts, axis=1)
    weight_grads = [
        jnp.dot(act_a.T, grads[k], preferred_element_type=F32).astype(BF16) for k in range(3)
    ]
    last = halves_sum(jnp.stack(weight_grads[:2]), jnp.stack([weight_grads[2], grad_attn_out_t]), dp)
    grad_act_a = jnp.einsum("cte,cde->td", grads, query_key_value_weight, preferred_element_type=F32)
    grad_table = offset_table_grad(bands, bucket, position_bias_matrix.shape[0])
    back_attn = pair_sum(grad_act_a.astype(BF16), tp)
    grad_in_part, grad_gain_attn = norm_back(back_attn, inputs, inverse_a, gain_attn)
    grad_tokens = (grad_hidden + grad_in_part).reshape(seqs, length, width)
    small = jnp.concatenate(
        [grad_gain_attn, grad_gain_expert, grad_router.T.reshape(-1), grad_table.reshape(-1)]
    )
    small = small_sum(small, dp)
    me = lax.axis_index("dp")
    share = width // dp
    wide = lax.dynamic_slice_in_dim(small[: 6 * width].reshape(6, width), me * share, share, axis=1)
    return (
        output,
        grad_tokens,
        wide[0],
        last[:3],
        last[3].T,
        small[6 * width :].reshape(position_bias_matrix.shape),
        wide[1],
        wide[2:].T,
        summed_in,
        jnp.transpose(summed_out, (0, 2, 1)),
    )


def solution(mesh):
    in_specs = (
        P("dp", None, None),
        P(),
        P(None, None, "tensor"),
        P("tensor", None),
        P(None, "tensor"),
        P(),
        P(),
        P(None, None, "tensor"),
        P(None, "tensor", None),
        P("dp", None),
        P("dp", None),
        P("dp", None),
        P("dp", None, None),
    )
    out_specs = (
        P("dp", None, None),
        P("dp", None, None),
        P("dp"),
        P(None, "dp", "tensor"),
        P("tensor", "dp"),
        P(None, "tensor"),
        P("dp"),
        P("dp", None),
        P(None, "dp", "tensor"),
        P(None, "tensor", "dp"),
    )
    run = functools.partial(body, mesh.shape["dp"], mesh.shape["tensor"])
    return jax.shard_map(run, mesh=mesh, in_specs=in_specs, out_specs=out_specs, check_vma=False)
```
